32 devices in a mesh: dom: 8 (over z, x), sub: 4 (over y, core).
Axes of the slice: x: 2, y: 2, z: 4, core: 2. Of those that a mesh axis runs over, the one named last changes fastest.
Arguments:
- excitation: bfloat16 [8, 1536, 64], P('dom', 'sub'), may hold values from -6 to 6
- local_inverse: bfloat16 [8, 1536, 1536], P('dom', 'sub'), as said below
- aggregation: bfloat16 [8, 1024, 1536], P('dom', None, 'sub'), may hold values from -0.15625 to 0.15625
- disaggregation: bfloat16 [8, 1536, 1024], P('dom', 'sub'), may hold values from -0.1875 to 0.1875
- translation: float32 [8, 6, 2, 512], P('dom'), may hold values from -1.5 to 1.5
- partners: int32 [8, 6], P('dom'), may hold values from 0 to 7, as said below
- list_counts: int32 [8], P('dom'), may hold values from 2 to 6
- sweep_order: int32 [8], replicated, may hold values from 0 to 7, as said below
Outputs:
- currents: float32 [8, 1536, 64], P('dom', 'sub')
The draws below stay inside these ranges and needn't reach their ends.
Inputs may be any that keep to these rules, and one draw needn't show every extreme that they name: `partners`: row d names 6 different subdomains, none equal to d; only its first list_counts[d] slots are used. `local_inverse`: each subdomain's matrix is the identity plus independent entries of spread 0.6 / sqrt(1536). `sweep_order`: every subdomain has a position of its own.
All inputs are finite; a program needn't handle non-finite values.
Results may differ from the reference program's by a relative error of at most 0.03.
Values may be sent and summed in bfloat16 or wider, within the bound.
A program may use at most 64 MiB of HBM per device.

```python
import jax
import jax.numpy as jnp
from jax import lax

U = 1536
R = 64
Q = 512
L = 6
SEGMENTS = 8
P2 = 1024
NDOM = 8


def draw_local_inverse(key, part):
    spread = 0.6 / U ** 0.5
    noise = jax.random.normal(key, (NDOM, U, U), jnp.float32)
    row_ids = jnp.arange(U, dtype=jnp.int32)
    identity = (row_ids[:, None] == row_ids[None, :]).astype(jnp.float32)
    return (identity[None, :, :] + spread * noise).astype(jnp.bfloat16)


def sweep_positions(key):
    return jax.random.permutation(jax.random.fold_in(key, 29), NDOM).astype(jnp.int32)


def draw_sweep_order(key, part):
    return sweep_positions(key)


def draw_partners(key, part):
    positions = sweep_positions(key)
    holders = jnp.argsort(positions).astype(jnp.int32)
    members = NDOM // SEGMENTS
    offsets = members + jnp.arange(L, dtype=jnp.int32)
    earlier = (positions[:, None] - offsets[None, :]) % NDOM
    return holders[earlier].astype(jnp.int32)


def plant(result, key, least, largest):
    shape = result.shape
    index_at = [jax.random.randint(jax.random.fold_in(key, axis), (), 0, shape[axis]) for axis in range(len(shape))]
    result = result.at[tuple(index_at)].set(least)
    longest = shape.index(max(shape))
    index_at[longest] = (index_at[longest] + 1) % shape[longest]
    return result.at[tuple(index_at)].set(largest)


def shard_levels(own_key, shape, shards, least, high):
    gain = 1.0
    for dim, shards_of in shards:
        heights = jax.random.uniform(jax.random.fold_in(jax.random.fold_in(own_key, 6), dim), (shards_of,), jnp.float32, least / len(shards), high / len(shards))
        gain = gain * jnp.repeat(jnp.exp(heights), shape[dim] // shards_of).reshape((-1,) + (1,) * (len(shape) - 1 - dim))
    return gain


def normal_values(own_key, shape, scale, bound, cuts=(), held_as=jnp.bfloat16):
    entries = jax.random.normal(own_key, shape, jnp.float32) * scale
    if len(cuts) > 0:
        entries = shard_levels(own_key, shape, cuts, -0.22, 0.18) * entries
    return jnp.clip(entries, min=-bound, max=bound).astype(held_as)


def setup_inputs(seed: int = 0) -> dict:
    key_list = jax.random.split(jax.random.key(seed), 9)
    return {
        "excitation": normal_values(key_list[0], (NDOM, U, R), 1.0, 6.0, ((0, 8), (1, 4))),
        "local_inverse": draw_local_inverse(jax.random.fold_in(key_list[8], 71), 0),
        "aggregation": normal_values(key_list[2], (NDOM, P2, U), U ** -0.5, 0.15625, ((0, 8), (2, 4))),
        "disaggregation": normal_values(key_list[3], (NDOM, U, P2), P2 ** -0.5, 0.1875, ((0, 8), (1, 4))),
        "translation": normal_values(key_list[4], (NDOM, L, 2, Q), 0.3, 1.5, ((0, 8),), jnp.float32),
        "partners": draw_partners(jax.random.fold_in(key_list[8], 71), 0),
        "list_counts": plant(jax.random.randint(key_list[6], (NDOM,), 2, L + 1), jax.random.fold_in(key_list[6], 1), 2, L).astype(jnp.int32),
        "sweep_order": draw_sweep_order(jax.random.fold_in(key_list[8], 71), 0),
    }


CONTRACT_FIRST = (((0,), (1,)), ((), ()))
CONTRACT_LAST = (((1,), (1,)), ((), ()))


def rotate(real_weight, imag_weight, pattern):
    samples = real_weight.shape[-1]
    values = pattern.astype(jnp.float32)
    real_part = values[..., :samples]
    imag_part = values[..., samples:]
    return jnp.concatenate([real_weight * real_part - imag_weight * imag_part, real_weight * imag_part + imag_weight * real_part], axis=-1)


def prepare(blocks):
    inverse_block, disagg_block, agg_block, excite_block = blocks
    solved = jnp.dot(inverse_block, excite_block, preferred_element_type=jnp.float32)
    solved_half = solved.astype(jnp.bfloat16)
    incident = lax.dot_general(solved_half, agg_block, CONTRACT_FIRST, preferred_element_type=jnp.float32)
    spread_half = jnp.dot(inverse_block, disagg_block, preferred_element_type=jnp.float32).astype(jnp.bfloat16)
    coupling = lax.dot_general(spread_half, agg_block, CONTRACT_FIRST, preferred_element_type=jnp.float32).astype(jnp.bfloat16)
    return solved, incident, spread_half, coupling


def finish(blocks):
    solved_block, spread_block, field_block = blocks
    return solved_block - lax.dot_general(spread_block, field_block, CONTRACT_LAST, preferred_element_type=jnp.float32)


def reference(excitation, local_inverse, aggregation, disaggregation, translation, partners, list_counts, sweep_order):
    solved, incident, spread_half, coupling = lax.map(prepare, (local_inverse, disaggregation, aggregation, excitation))
    domains = sweep_order.shape[0]
    segment_of = (sweep_order * SEGMENTS) // domains
    slot_ids = jnp.arange(partners.shape[1], dtype=jnp.int32)
    patterns = jnp.zeros(incident.shape, jnp.bfloat16)
    fields = jnp.zeros(incident.shape, jnp.bfloat16)
    for segment_k in range(SEGMENTS):
        live = (slot_ids[None, :] < list_counts[:, None]) & (segment_of[partners] < segment_k)
        weights = jnp.where(live[:, :, None, None], translation, jnp.zeros_like(translation))

        def gather_field(blocks):
            weight_block, linked = blocks
            terms = rotate(weight_block[:, 0][:, None, :], weight_block[:, 1][:, None, :], patterns[linked])
            return jnp.sum(terms, axis=0).astype(jnp.bfloat16)

        now_fields = lax.map(gather_field, (weights, partners))

        def radiate(blocks):
            field_block, incident_block, coupling_block = blocks
            return (incident_block - jnp.dot(field_block, coupling_block, preferred_element_type=jnp.float32)).astype(jnp.bfloat16)

        now_patterns = lax.map(radiate, (now_fields, incident, coupling))
        in_segment = (segment_of == segment_k)[:, None, None]
        fields = jnp.where(in_segment, now_fields, fields)
        patterns = jnp.where(in_segment, now_patterns, patterns)
    return lax.map(finish, (solved, spread_half, fields))
```

```python
import functools

import jax
import jax.numpy as jnp
from jax import lax
from jax.experimental import pallas as pl
from jax.experimental.pallas import tpu as pltpu
from jax.sharding import PartitionSpec as P

SEGMENTS = 8
CHUNKS = 4
MESH = pl.DeviceIdType.MESH
F32 = jnp.float32
BF16 = jnp.bfloat16


def each(lo, hi, body):
    if hi - lo <= 8:
        for i in range(lo, hi):
            body(i)
    else:
        lax.fori_loop(lo, hi, lambda i, c: (body(i), c)[1], 0)


def kernel(
    n,
    exc_ref, inv_ref, agg_ref, dis_ref, w_ref,
    out_ref,
    exc_all, dis_all, agg_t, solved, inc_part, inc_recv, inc, spread,
    pm, ps_recv, ps, py_recv, coup, pat, recv, field_all,
    exc_s, exc_r, dp_s, dp_r, ds_s, ds_r, dr_s, dr_r, inc_s, inc_r,
    pm_s, pm_r, py_s, py_r, cs_s, cs_r, pat_s, pat_r, fld_s, fld_r,
):
    me = lax.axis_index("dom")
    sub = lax.axis_index("sub")
    core = lax.rem(sub, 2)
    sib = sub + 1 - 2 * core
    peer = lax.rem(sub + 2, 4)
    rows = exc_ref.shape[0]
    wide = dis_ref.shape[1]
    cols = wide // CHUNKS
    half = cols // 2
    rhs = exc_ref.shape[1]
    part = rhs // 4
    q = wide // 2

    barrier = pltpu.get_barrier_semaphore()
    for off in range(1, 4):
        pl.semaphore_signal(barrier, inc=1, device_id={"sub": lax.rem(sub + off, 4)}, device_id_type=MESH)
    each(1, n, lambda off: pl.semaphore_signal(
        barrier, inc=1, device_id={"dom": lax.rem(me + off, n)}, device_id_type=MESH))
    pl.semaphore_wait(barrier, n + 2)

    def to_sub(src, dst, ss, rs, t):
        return pltpu.make_async_remote_copy(
            src_ref=src, dst_ref=dst, send_sem=ss, recv_sem=rs, device_id={"sub": t}, device_id_type=MESH)

    exc_copies = [
        to_sub(exc_ref, exc_all.at[off - 1], exc_s.at[off - 1], exc_r.at[off - 1], lax.rem(sub + off, 4))
        for off in range(1, 4)
    ]
    for c in exc_copies:
        c.start()

    def cut(j):
        return pl.ds(j * cols, cols)

    dp = [to_sub(dis_ref.at[:, cut(j)], dis_all.at[1, :, cut(j)], dp_s.at[j], dp_r.at[j], peer) for j in range(CHUNKS)]
    ds = [to_sub(dis_ref.at[:, cut(j)], dis_all.at[0, :, cut(j)], ds_s.at[j], ds_r.at[j], sib) for j in range(CHUNKS)]
    dr = [to_sub(dis_all.at[1, :, cut(j)], dis_all.at[2, :, cut(j)], dr_s.at[j], dr_r.at[j], sib) for j in range(CHUNKS)]
    for j in range(CHUNKS):
        dp[j].start()
        ds[j].start()

    agg_t[...] = agg_ref[...].T

    def inverse_columns(t):
        return inv_ref[:, pl.ds(pl.multiple_of(t * rows, 128), rows)]

    acc = jnp.dot(inverse_columns(sub), exc_ref[...], preferred_element_type=F32)
    for off in range(1, 4):
        exc_copies[off - 1].wait_recv()
        acc += jnp.dot(inverse_columns(lax.rem(sub + 4 - off, 4)), exc_all[off - 1], preferred_element_type=F32)
    solved[...] = acc
    inc_part[...] = jnp.dot(acc.T.astype(BF16), agg_t[...], preferred_element_type=F32).astype(BF16)

    def inc_rows(t):
        return inc_part.at[pl.ds(pl.multiple_of(t * part, 16), part), :]

    inc_copies = [
        to_sub(inc_rows(lax.rem(sub + off, 4)), inc_recv.at[off - 1], inc_s.at[off - 1], inc_r.at[off - 1], lax.rem(sub + off, 4))
        for off in range(1, 4)
    ]
    for c in inc_copies:
        c.start()

    mine = pl.multiple_of(core * half, half)
    other = pl.multiple_of((1 - core) * half, half)
    pmc = [to_sub(pm.at[j, pl.ds(other, half), :], ps_recv.at[j], pm_s.at[j], pm_r.at[j], sib) for j in range(CHUNKS)]
    pyc = [to_sub(ps.at[j], py_recv.at[j], py_s.at[j], py_r.at[j], peer) for j in range(CHUNKS)]
    own = [coup.at[pl.ds(pl.multiple_of(j * cols + core * half, half), half), :] for j in range(CHUNKS)]
    csc = [to_sub(own[j], own[j], cs_s.at[j], cs_r.at[j], sib) for j in range(CHUNKS)]

    def relay(j):
        dp[j].wait_recv()
        dr[j].start()

    def product(j):
        ds[j].wait_recv()
        dr[j].wait_recv()
        far = sib + 2 - 4 * (sib // 2)
        total = jnp.dot(inverse_columns(sub), dis_ref[:, cut(j)], preferred_element_type=F32)
        total += jnp.dot(inverse_columns(sib), dis_all[0, :, cut(j)], preferred_element_type=F32)
        total += jnp.dot(inverse_columns(peer), dis_all[1, :, cut(j)], preferred_element_type=F32)
        total += jnp.dot(inverse_columns(far), dis_all[2, :, cut(j)], preferred_element_type=F32)
        spread[:, cut(j)] = total.astype(BF16)
        pm[j] = jnp.dot(total.T.astype(BF16), agg_t[...], preferred_element_type=F32).astype(BF16)
        pmc[j].start()

    def pair(j):
        pmc[j].wait_recv()
        ps[j] = (pm[j, pl.ds(mine, half), :].astype(F32) + ps_recv[j].astype(F32)).astype(BF16)
        pyc[j].start()

    def finish(j):
        pyc[j].wait_recv()
        own[j][...] = (ps[j].astype(F32) + py_recv[j].astype(F32)).astype(BF16)
        csc[j].start()

    relay(0)
    for t in range(CHUNKS + 2):
        if t < CHUNKS:
            if t + 1 < CHUNKS:
                product(t)
                relay(t + 1)
            else:
                product(t)
        if 0 <= t - 1 < CHUNKS:
            pair(t - 1)
        if t == 1:
            total = inc_rows(sub)[...].astype(F32)
            for off in range(1, 4):
                inc_copies[off - 1].wait_recv()
                total += inc_recv[off - 1].astype(F32)
            inc[...] = total
            pat[0] = total.astype(BF16)
        if 0 <= t - 2 < CHUNKS:
            finish(t - 2)
    for j in range(CHUNKS):
        csc[j].wait_recv()

    def pattern_copy(slot, off):
        return pltpu.make_async_remote_copy(
            src_ref=pat.at[slot], dst_ref=recv.at[slot, off - 1],
            send_sem=pat_s.at[slot, off - 1], recv_sem=pat_r.at[slot, off - 1],
            device_id={"dom": lax.rem(me + off, n)}, device_id_type=MESH)

    def exchange(slot):
        each(1, n, lambda off: pattern_copy(slot, off).start())

        def term(off):
            pattern_copy(slot, off).wait()
            e = lax.rem(me + n - off, n)
            wr, wi = w_ref[e, 0:1, :], w_ref[e, 1:2, :]
            p = recv[slot, off - 1].astype(F32)
            pr, pi = p[:, :q], p[:, q:]
            return wr * pr - wi * pi, wr * pi + wi * pr

        zero = jnp.zeros((part, q), F32)
        if n <= 8:
            fr, fi = zero, zero
            for off in range(1, n):
                a, b = term(off)
                fr, fi = fr + a, fi + b
        else:
            def body(off, c):
                a, b = term(off)
                return c[0] + a, c[1] + b
            fr, fi = lax.fori_loop(1, n, body, (zero, zero))
        return jnp.concatenate([fr, fi], axis=1).astype(BF16)

    def step(k, carry):
        slot = lax.rem(k, 2)
        field = exchange(slot)
        pat[1 - slot] = (inc[...] - jnp.dot(field, coup[...], preferred_element_type=F32)).astype(BF16)
        return carry

    lax.fori_loop(0, SEGMENTS - 2, step, 0)
    field = exchange((SEGMENTS - 2) % 2)

    def field_rows(t):
        return field_all.at[pl.ds(pl.multiple_of(t * part, 16), part), :]

    field_rows(sub)[...] = field
    fld = [
        to_sub(field_rows(sub), field_rows(sub), fld_s.at[off - 1], fld_r.at[off - 1], lax.rem(sub + off, 4))
        for off in range(1, 4)
    ]
    for c in fld:
        c.start()
    for c in fld:
        c.wait_recv()
    out_ref[...] = solved[...] - lax.dot_general(
        spread[...], field_all[...], (((1,), (1,)), ((), ())), preferred_element_type=F32)

    for c in exc_copies + inc_copies + dp + ds + dr + pmc + pyc + csc + fld:
        c.wait_send()


def local(
    n, excitation, local_inverse, aggregation, disaggregation, translation, partners, list_counts, sweep_order
):
    domains = sweep_order.shape[0]
    segment_of = sweep_order * SEGMENTS // domains
    my_segment = segment_of[lax.axis_index("dom")]
    row = partners[0]
    live = jnp.arange(row.shape[0], dtype=jnp.int32) < list_counts[0]
    ids = jnp.arange(domains, dtype=jnp.int32)
    match = (row[:, None] == ids[None, :]) & live[:, None] & (segment_of < my_segment)[None, :]
    weights = jnp.sum(jnp.where(match[:, :, None, None], translation[0][:, None], 0.0), axis=0)

    rows, rhs = excitation.shape[1:]
    wide = disaggregation.shape[2]
    cols = wide // CHUNKS
    part = rhs // 4
    dma = lambda *s: pltpu.SemaphoreType.DMA(s)
    vm = pl.BlockSpec(memory_space=pltpu.VMEM)
    out = pl.pallas_call(
        functools.partial(kernel, n),
        out_shape=jax.ShapeDtypeStruct((rows, rhs), F32),
        in_specs=[vm] * 5,
        out_specs=vm,
        scratch_shapes=[
            pltpu.VMEM((3, rows, rhs), BF16),
            pltpu.VMEM((3, rows, wide), BF16),
            pltpu.VMEM((rows, wide), BF16),
            pltpu.VMEM((rows, rhs), F32),
            pltpu.VMEM((rhs, wide), BF16),
            pltpu.VMEM((3, part, wide), BF16),
            pltpu.VMEM((part, wide), F32),
            pltpu.VMEM((rows, wide), BF16),
            pltpu.VMEM((CHUNKS, cols, wide), BF16),
            pltpu.VMEM((CHUNKS, cols // 2, wide), BF16),
            pltpu.VMEM((CHUNKS, cols // 2, wide), BF16),
            pltpu.VMEM((CHUNKS, cols // 2, wide), BF16),
            pltpu.VMEM((wide, wide), BF16),
            pltpu.VMEM((2, part, wide), BF16),
            pltpu.VMEM((2, n - 1, part, wide), BF16),
            pltpu.VMEM((rhs, wide), BF16),
            dma(3), dma(3),
            dma(CHUNKS), dma(CHUNKS), dma(CHUNKS), dma(CHUNKS), dma(CHUNKS), dma(CHUNKS),
            dma(3), dma(3),
            dma(CHUNKS), dma(CHUNKS), dma(CHUNKS), dma(CHUNKS), dma(CHUNKS), dma(CHUNKS),
            dma(2, n - 1), dma(2, n - 1),
            dma(3), dma(3),
        ],
        compiler_params=pltpu.CompilerParams(
            collective_id=0, has_side_effects=True, vmem_limit_bytes=48 * 1024 * 1024
        ),
    )(excitation[0], local_inverse[0], aggregation[0], disaggregation[0], weights)
    return out[None]


def solution(mesh):
    in_specs = (
        P("dom", "sub", None),
        P("dom", "sub", None),
        P("dom", None, "sub"),
        P("dom", "sub", None),
        P("dom", None, None, None),
        P("dom", None),
        P("dom"),
        P(),
    )
    out_specs = P("dom", "sub", None)
    return jax.shard_map(
        functools.partial(local, mesh.shape["dom"]),
        mesh=mesh, in_specs=in_specs, out_specs=out_specs, check_vma=False,
    )
```

```python
import functools

import jax
import jax.numpy as jnp
from jax import lax
from jax.experimental import pallas as pl
from jax.experimental.pallas import tpu as pltpu
from jax.sharding import PartitionSpec as P

SEGMENTS = 8
CHUNKS = 4
MESH = pl.DeviceIdType.MESH
F32 = jnp.float32
BF16 = jnp.bfloat16


def each(lo, hi, body):
    if hi - lo <= 8:
        for i in range(lo, hi):
            body(i)
    else:
        lax.fori_loop(lo, hi, lambda i, c: (body(i), c)[1], 0)


def kernel(
    n,
    exc_ref, inv_hbm, agg_hbm, dis_hbm, trans_ref, partners_ref, count_ref, order_ref,
    out_ref,
    inv_ref, agg_ref, dis_ref,
    exc_all, dis_all, agg_t, solved_t, inc_part, inc_recv, inc, spread_t,
    pm, ps_recv, ps, py_recv, coup, w, facc,
    pat_a, pat_b, xa_recv, xb_recv, merged_a, merged_b, za_recv, zb_recv, field_all,
    load_s,
    exc_s, exc_r, dp_s, dp_r, ds_s, ds_r, dr_s, dr_r, inc_s, inc_r,
    pm_s, pm_r, py_s, py_r, cs_s, cs_r, xa_s, xa_r, xb_s, xb_r, za_s, za_r, zb_s, zb_r, fld_s, fld_r,
):
    me = lax.axis_index("dom")
    sub = lax.axis_index("sub")
    core = lax.rem(sub, 2)
    sib = sub + 1 - 2 * core
    peer = lax.rem(sub + 2, 4)
    rhs, rows = exc_ref.shape
    wide = dis_ref.shape[1]
    cols = wide // CHUNKS
    half = cols // 2
    part = rhs // 4
    q = wide // 2
    members = n // SEGMENTS
    line = n // 2
    fast = lax.rem(me, 2)
    slow = me // 2

    loads = [
        pltpu.make_async_copy(src, dst, load_s.at[i])
        for i, (src, dst) in enumerate([(inv_hbm, inv_ref), (agg_hbm, agg_ref), (dis_hbm, dis_ref)])
    ]
    for c in loads:
        c.start()

    barrier = pltpu.get_barrier_semaphore()
    for off in range(1, 4):
        pl.semaphore_signal(barrier, inc=1, device_id={"sub": lax.rem(sub + off, 4)}, device_id_type=MESH)
    each(1, n, lambda off: pl.semaphore_signal(
        barrier, inc=1, device_id={"dom": lax.rem(me + off, n)}, device_id_type=MESH))
    pl.semaphore_wait(barrier, n + 2)

    def to_sub(src, dst, ss, rs, t):
        return pltpu.make_async_remote_copy(
            src_ref=src, dst_ref=dst, send_sem=ss, recv_sem=rs, device_id={"sub": t}, device_id_type=MESH)

    exc_copies = [
        to_sub(exc_ref, exc_all.at[off - 1], exc_s.at[off - 1], exc_r.at[off - 1], lax.rem(sub + off, 4))
        for off in range(1, 4)
    ]
    for c in exc_copies:
        c.start()

    def cut(j):
        return pl.ds(j * cols, cols)

    dp = [to_sub(dis_hbm.at[:, cut(j)], dis_all.at[1, :, cut(j)], dp_s.at[j], dp_r.at[j], peer) for j in range(CHUNKS)]
    ds = [to_sub(dis_hbm.at[:, cut(j)], dis_all.at[0, :, cut(j)], ds_s.at[j], ds_r.at[j], sib) for j in range(CHUNKS)]
    dr = [to_sub(dis_all.at[1, :, cut(j)], dis_all.at[2, :, cut(j)], dr_s.at[j], dr_r.at[j], sib) for j in range(CHUNKS)]
    for j in range(CHUNKS):
        dp[j].start()
        ds[j].start()

    my_pos = order_ref[me]
    slots = partners_ref.shape[0]
    slot_pos = [jnp.where(l < count_ref[0], order_ref[partners_ref[l]], -1) for l in range(slots)]

    def weigh(p):
        earlier = p // members < my_pos // members
        total = jnp.zeros((2, q), F32)
        for l in range(slots):
            total += jnp.where((slot_pos[l] == p) & earlier, 1.0, 0.0) * trans_ref[l]
        w[p] = total

    each(0, n - members, weigh)

    loads[1].wait()
    agg_t[...] = agg_ref[...].T
    loads[0].wait()
    loads[2].wait()

    def inverse_columns(t):
        return inv_ref[:, pl.ds(pl.multiple_of(t * rows, 128), rows)]

    def apply(block, t):
        return lax.dot_general(block, inverse_columns(t), (((1,), (1,)), ((), ())), preferred_element_type=F32)

    acc = apply(exc_ref[...], sub)
    for off in range(1, 4):
        exc_copies[off - 1].wait_recv()
        acc += apply(exc_all[off - 1], lax.rem(sub + 4 - off, 4))
    solved_t[...] = acc
    inc_part[...] = jnp.dot(acc.astype(BF16), agg_t[...], preferred_element_type=F32).astype(BF16)

    def inc_rows(t):
        return inc_part.at[pl.ds(pl.multiple_of(t * part, 16), part), :]

    inc_copies = [
        to_sub(inc_rows(lax.rem(sub + off, 4)), inc_recv.at[off - 1], inc_s.at[off - 1], inc_r.at[off - 1], lax.rem(sub + off, 4))
        for off in range(1, 4)
    ]
    for c in inc_copies:
        c.start()

    mine = pl.multiple_of(core * half, half)
    other = pl.multiple_of((1 - core) * half, half)
    pmc = [to_sub(pm.at[j, pl.ds(other, half), :], ps_recv.at[j], pm_s.at[j], pm_r.at[j], sib) for j in range(CHUNKS)]
    pyc = [to_sub(ps.at[j], py_recv.at[j], py_s.at[j], py_r.at[j], peer) for j in range(CHUNKS)]
    own = [coup.at[pl.ds(pl.multiple_of(j * cols + core * half, half), half), :] for j in range(CHUNKS)]
    csc = [to_sub(own[j], own[j], cs_s.at[j], cs_r.at[j], sib) for j in range(CHUNKS)]

    def relay(j):
        dp[j].wait_recv()
        dr[j].start()

    def product(j):
        ds[j].wait_recv()
        dr[j].wait_recv()
        far = sib + 2 - 4 * (sib // 2)
        total = jnp.dot(inverse_columns(sub), dis_ref[:, cut(j)], preferred_element_type=F32)
        total += jnp.dot(inverse_columns(sib), dis_all[0, :, cut(j)], preferred_element_type=F32)
        total += jnp.dot(inverse_columns(peer), dis_all[1, :, cut(j)], preferred_element_type=F32)
        total += jnp.dot(inverse_columns(far), dis_all[2, :, cut(j)], preferred_element_type=F32)
        total = total.T.astype(BF16)
        spread_t[cut(j), :] = total
        pm[j] = jnp.dot(total, agg_t[...], preferred_element_type=F32).astype(BF16)
        pmc[j].start()

    def pair(j):
        pmc[j].wait_recv()
        ps[j] = (pm[j, pl.ds(mine, half), :].astype(F32) + ps_recv[j].astype(F32)).astype(BF16)
        pyc[j].start()

    def finish(j):
        pyc[j].wait_recv()
        own[j][...] = (ps[j].astype(F32) + py_recv[j].astype(F32)).astype(BF16)
        csc[j].start()

    def to_dom(src, dst, ss, rs, d):
        return pltpu.make_async_remote_copy(
            src_ref=src, dst_ref=dst, send_sem=ss, recv_sem=rs, device_id={"dom": d}, device_id_type=MESH)

    def short(src, dst, ss, rs, slot):
        return to_dom(src.at[slot], dst.at[slot], ss.at[slot], rs.at[slot], me + 1 - 2 * fast)

    def long(src, dst, ss, rs, slot, off):
        return to_dom(src.at[slot], dst.at[slot, off - 1], ss.at[slot, off - 1], rs.at[slot, off - 1],
                      2 * lax.rem(slow + off, line) + fast)

    xa = functools.partial(short, pat_a, xa_recv, xa_s, xa_r)
    xb = functools.partial(short, merged_b, xb_recv, xb_s, xb_r)
    za = functools.partial(long, merged_a, za_recv, za_s, za_r)
    zb = functools.partial(long, pat_b, zb_recv, zb_s, zb_r)

    def put(dst, slot, k, values):
        place = jnp.full(values.shape, my_pos, jnp.int32)
        for m in range(members):
            dst[slot, m * part:(m + 1) * part, :] = jnp.where(
                place == k * members + m, values, 0.0).astype(BF16)

    def gather(copies, own, recv, slot):
        total = own[slot].astype(F32)
        if line <= 8:
            for off in range(1, line):
                copies(slot, off).wait()
                total += recv[slot, off - 1].astype(F32)
            return total

        def body(off, c):
            copies(slot, off).wait()
            return c + recv[slot, off - 1].astype(F32)
        return lax.fori_loop(1, line, body, total)

    def begin(slot, k, first, second):
        put(pat_a, slot, k, first())
        xa(slot).start()
        put(pat_b, slot, k, second())
        each(1, line, lambda off: zb(slot, off).start())

    def turn_a(slot):
        xa(slot).wait()
        merged_a[slot] = (pat_a[slot].astype(F32) + xa_recv[slot].astype(F32)).astype(BF16)
        each(1, line, lambda off: za(slot, off).start())

    def turn_b(slot):
        merged_b[slot] = gather(zb, pat_b, zb_recv, slot).astype(BF16)
        xb(slot).start()

    def end(slot, k):
        real = gather(za, merged_a, za_recv, slot)
        xb(slot).wait()
        imag = merged_b[slot].astype(F32) + xb_recv[slot].astype(F32)
        fr, fi = facc[0], facc[1]
        for m in range(members):
            wr, wi = w[k * members + m, 0:1, :], w[k * members + m, 1:2, :]
            pr, pi = real[m * part:(m + 1) * part], imag[m * part:(m + 1) * part]
            fr += wr * pr - wi * pi
            fi += wr * pi + wi * pr
        facc[0] = fr
        facc[1] = fi

    def field_now():
        return jnp.concatenate([facc[0], facc[1]], axis=1).astype(BF16)

    facc[...] = jnp.zeros(facc.shape, F32)
    relay(0)
    for t in range(CHUNKS + 2):
        if t < CHUNKS:
            product(t)
            if t + 1 < CHUNKS:
                relay(t + 1)
        if 0 <= t - 1 < CHUNKS:
            pair(t - 1)
        if t == 1:
            total = inc_rows(sub)[...].astype(F32)
            for off in range(1, 4):
                inc_copies[off - 1].wait_recv()
                total += inc_recv[off - 1].astype(F32)
            inc[...] = total
            begin(0, 0, lambda: inc[:, :q], lambda: inc[:, q:])
        if t == 2:
            turn_a(0)
        if t == 3:
            turn_b(0)
        if t == 4:
            end(0, 0)
        if 0 <= t - 2 < CHUNKS:
            finish(t - 2)
    for j in range(CHUNKS):
        csc[j].wait_recv()

    def step(k, carry):
        slot = lax.rem(k, 2)
        field = field_now()

        def columns(lo):
            return inc[:, lo:lo + q] - jnp.dot(field, coup[:, lo:lo + q], preferred_element_type=F32)

        begin(slot, k, lambda: columns(0), lambda: columns(q))
        turn_a(slot)
        turn_b(slot)
        end(slot, k)
        return carry

    lax.fori_loop(1, SEGMENTS - 1, step, 0)
    field = field_now()

    def field_rows(t):
        return field_all.at[pl.ds(pl.multiple_of(t * part, 16), part), :]

    field_rows(sub)[...] = field
    fld = [
        to_sub(field_rows(sub), field_rows(sub), fld_s.at[off - 1], fld_r.at[off - 1], lax.rem(sub + off, 4))
        for off in range(1, 4)
    ]
    for c in fld:
        c.start()
    for c in fld:
        c.wait_recv()
    out_ref[...] = solved_t[...] - jnp.dot(field_all[...], spread_t[...], preferred_element_type=F32)

    for c in exc_copies + inc_copies + dp + ds + dr + pmc + pyc + csc + fld:
        c.wait_send()


def local(
    n, excitation, local_inverse, aggregation, disaggregation, translation, partners, list_counts, sweep_order
):
    rows, rhs = excitation.shape[1:]
    wide = disaggregation.shape[2]
    cols = wide // CHUNKS
    part = rhs // 4
    stack = n // SEGMENTS * part
    line = n // 2
    dma = lambda *s: pltpu.SemaphoreType.DMA(s)
    vm = pl.BlockSpec(memory_space=pltpu.VMEM)
    sm = pl.BlockSpec(memory_space=pltpu.SMEM)
    hbm = pl.BlockSpec(memory_space=pl.ANY)
    out = pl.pallas_call(
        functools.partial(kernel, n),
        out_shape=jax.ShapeDtypeStruct((rhs, rows), F32),
        in_specs=[vm, hbm, hbm, hbm, vm, sm, sm, sm],
        out_specs=vm,
        scratch_shapes=[
            pltpu.VMEM(local_inverse.shape[1:], BF16),
            pltpu.VMEM(aggregation.shape[1:], BF16),
            pltpu.VMEM((rows, wide), BF16),
            pltpu.VMEM((3, rhs, rows), BF16),
            pltpu.VMEM((3, rows, wide), BF16),
            pltpu.VMEM((rows, wide), BF16),
            pltpu.VMEM((rhs, rows), F32),
            pltpu.VMEM((rhs, wide), BF16),
            pltpu.VMEM((3, part, wide), BF16),
            pltpu.VMEM((part, wide), F32),
            pltpu.VMEM((wide, rows), BF16),
            pltpu.VMEM((CHUNKS, cols, wide), BF16),
            pltpu.VMEM((CHUNKS, cols // 2, wide), BF16),
            pltpu.VMEM((CHUNKS, cols // 2, wide), BF16),
            pltpu.VMEM((CHUNKS, cols // 2, wide), BF16),
            pltpu.VMEM((wide, wide), BF16),
            pltpu.VMEM((n, 2, wide // 2), F32),
            pltpu.VMEM((2, part, wide // 2), F32),
            *[pltpu.VMEM((2, stack, wide // 2), BF16)] * 6,
            *[pltpu.VMEM((2, line - 1, stack, wide // 2), BF16)] * 2,
            pltpu.VMEM((rhs, wide), BF16),
            dma(3),
            dma(3), dma(3),
            dma(CHUNKS), dma(CHUNKS), dma(CHUNKS), dma(CHUNKS), dma(CHUNKS), dma(CHUNKS),
            dma(3), dma(3),
            dma(CHUNKS), dma(CHUNKS), dma(CHUNKS), dma(CHUNKS), dma(CHUNKS), dma(CHUNKS),
            dma(2), dma(2), dma(2), dma(2),
            *[dma(2, line - 1)] * 4,
            dma(3), dma(3),
        ],
        compiler_params=pltpu.CompilerParams(
            collective_id=0, has_side_effects=True, vmem_limit_bytes=56 * 1024 * 1024
        ),
    )(
        excitation[0].T, local_inverse[0], aggregation[0], disaggregation[0],
        translation[0], partners[0], list_counts, sweep_order,
    )
    return out.T[None]


def solution(mesh):
    in_specs = (
        P("dom", "sub", None),
        P("dom", "sub", None),
        P("dom", None, "sub"),
        P("dom", "sub", None),
        P("dom", None, None, None),
        P("dom", None),
        P("dom"),
        P(),
    )
    out_specs = P("dom", "sub", None)
    return jax.shard_map(
        functools.partial(local, mesh.shape["dom"]),
        mesh=mesh, in_specs=in_specs, out_specs=out_specs, check_vma=False,
    )
```

```python
import functools

import jax
import jax.numpy as jnp
from jax import lax
from jax.experimental import pallas as pl
from jax.experimental.pallas import tpu as pltpu
from jax.sharding import PartitionSpec as P

SEGMENTS = 8
CHUNKS = 4
MESH = pl.DeviceIdType.MESH
F32 = jnp.float32
BF16 = jnp.bfloat16


def each(lo, hi, body):
    if hi - lo <= 8:
        for i in range(lo, hi):
            body(i)
    else:
        lax.fori_loop(lo, hi, lambda i, c: (body(i), c)[1], 0)


def kernel(
    n,
    exc_ref, inv_hbm, agg_hbm, dis_hbm, trans_ref, partners_ref, count_ref, order_ref,
    out_ref,
    inv_ref, agg_ref, dis_ref,
    exc_all, dis_all, agg_t, solved_t, inc_part, inc_recv, inc, spread_t,
    pm, ps_recv, ps, py_recv, coup, w, facc,
    pat_a, pat_b, xa_recv, xb_recv, merged_a, merged_b, za_recv, zb_recv, field_all,
    load_s,
    exc_s, exc_r, dp_s, dp_r, ds_s, ds_r, dr_s, dr_r, inc_s, inc_r,
    pm_s, pm_r, py_s, py_r, cs_s, cs_r, xa_s, xa_r, xb_s, xb_r, za_s, za_r, zb_s, zb_r, fld_s, fld_r,
):
    me = lax.axis_index("dom")
    sub = lax.axis_index("sub")
    core = lax.rem(sub, 2)
    sib = sub + 1 - 2 * core
    peer = lax.rem(sub + 2, 4)
    rhs, rows = exc_ref.shape
    wide = dis_ref.shape[1]
    cols = wide // CHUNKS
    half = cols // 2
    part = rhs // 4
    q = wide // 2
    members = n // SEGMENTS
    line = n // 2
    fast = lax.rem(me, 2)
    slow = me // 2

    loads = [
        pltpu.make_async_copy(src, dst, load_s.at[i])
        for i, (src, dst) in enumerate([(inv_hbm, inv_ref), (agg_hbm, agg_ref), (dis_hbm, dis_ref)])
    ]
    for c in loads:
        c.start()

    barrier = pltpu.get_barrier_semaphore()
    for off in range(1, 4):
        pl.semaphore_signal(barrier, inc=1, device_id={"sub": lax.rem(sub + off, 4)}, device_id_type=MESH)
    each(1, n, lambda off: pl.semaphore_signal(
        barrier, inc=1, device_id={"dom": lax.rem(me + off, n)}, device_id_type=MESH))
    pl.semaphore_wait(barrier, n + 2)

    def to_sub(src, dst, ss, rs, t):
        return pltpu.make_async_remote_copy(
            src_ref=src, dst_ref=dst, send_sem=ss, recv_sem=rs, device_id={"sub": t}, device_id_type=MESH)

    exc_copies = [
        to_sub(exc_ref, exc_all.at[off - 1], exc_s.at[off - 1], exc_r.at[off - 1], lax.rem(sub + off, 4))
        for off in range(1, 4)
    ]
    for c in exc_copies:
        c.start()

    def cut(j):
        return pl.ds(j * cols, cols)

    dp = [to_sub(dis_hbm.at[:, cut(j)], dis_all.at[1, :, cut(j)], dp_s.at[j], dp_r.at[j], peer) for j in range(CHUNKS)]
    ds = [to_sub(dis_hbm.at[:, cut(j)], dis_all.at[0, :, cut(j)], ds_s.at[j], ds_r.at[j], sib) for j in range(CHUNKS)]
    dr = [to_sub(dis_all.at[1, :, cut(j)], dis_all.at[2, :, cut(j)], dr_s.at[j], dr_r.at[j], sib) for j in range(CHUNKS)]
    for j in range(CHUNKS):
        dp[j].start()
        ds[j].start()

    my_pos = order_ref[me]
    slots = partners_ref.shape[0]
    slot_pos = [jnp.where(l < count_ref[0], order_ref[partners_ref[l]], -1) for l in range(slots)]

    def weigh(p):
        earlier = p // members < my_pos // members
        total = jnp.zeros((2, q), F32)
        for l in range(slots):
            total += jnp.where((slot_pos[l] == p) & earlier, 1.0, 0.0) * trans_ref[l]
        w[p] = total

    each(0, n - members, weigh)

    loads[1].wait()
    agg_t[...] = agg_ref[...].T
    loads[0].wait()
    loads[2].wait()

    def inverse_columns(t):
        return inv_ref[:, pl.ds(pl.multiple_of(t * rows, 128), rows)]

    def apply(block, t):
        return lax.dot_general(block, inverse_columns(t), (((1,), (1,)), ((), ())), preferred_element_type=F32)

    acc = apply(exc_ref[...], sub)
    for off in range(1, 4):
        exc_copies[off - 1].wait_recv()
        acc += apply(exc_all[off - 1], lax.rem(sub + 4 - off, 4))
    solved_t[...] = acc
    inc_part[...] = jnp.dot(acc.astype(BF16), agg_t[...], preferred_element_type=F32).astype(BF16)

    def inc_rows(t):
        return inc_part.at[pl.ds(pl.multiple_of(t * part, 16), part), :]

    inc_copies = [
        to_sub(inc_rows(lax.rem(sub + off, 4)), inc_recv.at[off - 1], inc_s.at[off - 1], inc_r.at[off - 1], lax.rem(sub + off, 4))
        for off in range(1, 4)
    ]
    for c in inc_copies:
        c.start()

    mine = pl.multiple_of(core * half, half)
    other = pl.multiple_of((1 - core) * half, half)
    pmc = [to_sub(pm.at[j, pl.ds(other, half), :], ps_recv.at[j], pm_s.at[j], pm_r.at[j], sib) for j in range(CHUNKS)]
    pyc = [to_sub(ps.at[j], py_recv.at[j], py_s.at[j], py_r.at[j], peer) for j in range(CHUNKS)]
    own = [coup.at[pl.ds(pl.multiple_of(j * cols + core * half, half), half), :] for j in range(CHUNKS)]
    csc = [to_sub(own[j], own[j], cs_s.at[j], cs_r.at[j], sib) for j in range(CHUNKS)]

    def relay(j):
        dp[j].wait_recv()
        dr[j].start()

    def product(j):
        ds[j].wait_recv()
        dr[j].wait_recv()
        far = sib + 2 - 4 * (sib // 2)
        total = jnp.dot(inverse_columns(sub), dis_ref[:, cut(j)], preferred_element_type=F32)
        total += jnp.dot(inverse_columns(sib), dis_all[0, :, cut(j)], preferred_element_type=F32)
        total += jnp.dot(inverse_columns(peer), dis_all[1, :, cut(j)], preferred_element_type=F32)
        total += jnp.dot(inverse_columns(far), dis_all[2, :, cut(j)], preferred_element_type=F32)
        total = total.T.astype(BF16)
        spread_t[cut(j), :] = total
        pm[j] = jnp.dot(total, agg_t[...], preferred_element_type=F32).astype(BF16)
        pmc[j].start()

    def pair(j):
        pmc[j].wait_recv()
        ps[j] = (pm[j, pl.ds(mine, half), :].astype(F32) + ps_recv[j].astype(F32)).astype(BF16)
        pyc[j].start()

    def finish(j):
        pyc[j].wait_recv()
        own[j][...] = (ps[j].astype(F32) + py_recv[j].astype(F32)).astype(BF16)
        csc[j].start()

    def to_dom(src, dst, ss, rs, d):
        return pltpu.make_async_remote_copy(
            src_ref=src, dst_ref=dst, send_sem=ss, recv_sem=rs, device_id={"dom": d}, device_id_type=MESH)

    def short(src, dst, ss, rs, slot):
        return to_dom(src.at[slot], dst.at[slot], ss.at[slot], rs.at[slot], me + 1 - 2 * fast)

    def long(src, dst, ss, rs, slot, off):
        return to_dom(src.at[slot], dst.at[slot, off - 1], ss.at[slot, off - 1], rs.at[slot, off - 1],
                      2 * lax.rem(slow + off, line) + fast)

    xa = functools.partial(short, pat_a, xa_recv, xa_s, xa_r)
    xb = functools.partial(short, merged_b, xb_recv, xb_s, xb_r)
    za = functools.partial(long, merged_a, za_recv, za_s, za_r)
    zb = functools.partial(long, pat_b, zb_recv, zb_s, zb_r)

    def put(dst, slot, k, values):
        place = jnp.full(values.shape, my_pos, jnp.int32)
        for m in range(members):
            dst[slot, m * part:(m + 1) * part, :] = jnp.where(
                place == k * members + m, values, 0.0).astype(BF16)

    def gather(copies, own, recv, slot):
        total = own[slot].astype(F32)
        if line <= 8:
            for off in range(1, line):
                copies(slot, off).wait()
                total += recv[slot, off - 1].astype(F32)
            return total

        def body(off, c):
            copies(slot, off).wait()
            return c + recv[slot, off - 1].astype(F32)
        return lax.fori_loop(1, line, body, total)

    def begin(slot, k, first, second):
        put(pat_a, slot, k, first())
        xa(slot).start()
        put(pat_b, slot, k, second())
        each(1, line, lambda off: zb(slot, off).start())

    def turn_a(slot):
        xa(slot).wait()
        merged_a[slot] = (pat_a[slot].astype(F32) + xa_recv[slot].astype(F32)).astype(BF16)
        each(1, line, lambda off: za(slot, off).start())

    def turn_b(slot):
        merged_b[slot] = gather(zb, pat_b, zb_recv, slot).astype(BF16)
        xb(slot).start()

    def end(slot, k):
        real = gather(za, merged_a, za_recv, slot)
        xb(slot).wait()
        imag = merged_b[slot].astype(F32) + xb_recv[slot].astype(F32)
        fr, fi = facc[0], facc[1]
        for m in range(members):
            wr, wi = w[k * members + m, 0:1, :], w[k * members + m, 1:2, :]
            pr, pi = real[m * part:(m + 1) * part], imag[m * part:(m + 1) * part]
            fr += wr * pr - wi * pi
            fi += wr * pi + wi * pr
        facc[0] = fr
        facc[1] = fi

    def field_now():
        return jnp.concatenate([facc[0], facc[1]], axis=1).astype(BF16)

    facc[...] = jnp.zeros(facc.shape, F32)
    relay(0)
    for t in range(CHUNKS + 2):
        if t < CHUNKS:
            product(t)
            if t + 1 < CHUNKS:
                relay(t + 1)
            pair(t)
        if t == 1:
            total = inc_rows(sub)[...].astype(F32)
            for off in range(1, 4):
                inc_copies[off - 1].wait_recv()
                total += inc_recv[off - 1].astype(F32)
            inc[...] = total
            begin(0, 0, lambda: inc[:, :q], lambda: inc[:, q:])
        if t == 2:
            turn_a(0)
        if t == 3:
            turn_b(0)
        if t == 4:
            end(0, 0)
        if 0 <= t - 2 < CHUNKS:
            finish(t - 2)
    for j in range(CHUNKS):
        csc[j].wait_recv()

    def step(k, carry):
        slot = lax.rem(k, 2)
        field = field_now()

        def columns(lo):
            return inc[:, lo:lo + q] - jnp.dot(field, coup[:, lo:lo + q], preferred_element_type=F32)

        begin(slot, k, lambda: columns(0), lambda: columns(q))
        turn_a(slot)
        turn_b(slot)
        end(slot, k)
        return carry

    lax.fori_loop(1, SEGMENTS - 1, step, 0)
    field = field_now()

    def field_rows(t):
        return field_all.at[pl.ds(pl.multiple_of(t * part, 16), part), :]

    field_rows(sub)[...] = field
    fld = [
        to_sub(field_rows(sub), field_rows(sub), fld_s.at[off - 1], fld_r.at[off - 1], lax.rem(sub + off, 4))
        for off in range(1, 4)
    ]
    for c in fld:
        c.start()
    for c in fld:
        c.wait_recv()
    out_ref[...] = solved_t[...] - jnp.dot(field_all[...], spread_t[...], preferred_element_type=F32)

    for c in exc_copies + inc_copies + dp + ds + dr + pmc + pyc + csc + fld:
        c.wait_send()


def local(
    n, excitation, local_inverse, aggregation, disaggregation, translation, partners, list_counts, sweep_order
):
    rows, rhs = excitation.shape[1:]
    wide = disaggregation.shape[2]
    cols = wide // CHUNKS
    part = rhs // 4
    stack = n // SEGMENTS * part
    line = n // 2
    dma = lambda *s: pltpu.SemaphoreType.DMA(s)
    vm = pl.BlockSpec(memory_space=pltpu.VMEM)
    sm = pl.BlockSpec(memory_space=pltpu.SMEM)
    hbm = pl.BlockSpec(memory_space=pl.ANY)
    out = pl.pallas_call(
        functools.partial(kernel, n),
        out_shape=jax.ShapeDtypeStruct((rhs, rows), F32),
        in_specs=[vm, hbm, hbm, hbm, vm, sm, sm, sm],
        out_specs=vm,
        scratch_shapes=[
            pltpu.VMEM(local_inverse.shape[1:], BF16),
            pltpu.VMEM(aggregation.shape[1:], BF16),
            pltpu.VMEM((rows, wide), BF16),
            pltpu.VMEM((3, rhs, rows), BF16),
            pltpu.VMEM((3, rows, wide), BF16),
            pltpu.VMEM((rows, wide), BF16),
            pltpu.VMEM((rhs, rows), F32),
            pltpu.VMEM((rhs, wide), BF16),
            pltpu.VMEM((3, part, wide), BF16),
            pltpu.VMEM((part, wide), F32),
            pltpu.VMEM((wide, rows), BF16),
            pltpu.VMEM((CHUNKS, cols, wide), BF16),
            pltpu.VMEM((CHUNKS, cols // 2, wide), BF16),
            pltpu.VMEM((CHUNKS, cols // 2, wide), BF16),
            pltpu.VMEM((CHUNKS, cols // 2, wide), BF16),
            pltpu.VMEM((wide, wide), BF16),
            pltpu.VMEM((n, 2, wide // 2), F32),
            pltpu.VMEM((2, part, wide // 2), F32),
            *[pltpu.VMEM((2, stack, wide // 2), BF16)] * 6,
            *[pltpu.VMEM((2, line - 1, stack, wide // 2), BF16)] * 2,
            pltpu.VMEM((rhs, wide), BF16),
            dma(3),
            dma(3), dma(3),
            dma(CHUNKS), dma(CHUNKS), dma(CHUNKS), dma(CHUNKS), dma(CHUNKS), dma(CHUNKS),
            dma(3), dma(3),
            dma(CHUNKS), dma(CHUNKS), dma(CHUNKS), dma(CHUNKS), dma(CHUNKS), dma(CHUNKS),
            dma(2), dma(2), dma(2), dma(2),
            *[dma(2, line - 1)] * 4,
            dma(3), dma(3),
        ],
        compiler_params=pltpu.CompilerParams(
            collective_id=0, has_side_effects=True, vmem_limit_bytes=56 * 1024 * 1024
        ),
    )(
        excitation[0].T, local_inverse[0], aggregation[0], disaggregation[0],
        translation[0], partners[0], list_counts, sweep_order,
    )
    return out.T[None]


def solution(mesh):
    in_specs = (
        P("dom", "sub", None),
        P("dom", "sub", None),
        P("dom", None, "sub"),
        P("dom", "sub", None),
        P("dom", None, None, None),
        P("dom", None),
        P("dom"),
        P(),
    )
    out_specs = P("dom", "sub", None)
    return jax.shard_map(
        functools.partial(local, mesh.shape["dom"]),
        mesh=mesh, in_specs=in_specs, out_specs=out_specs, check_vma=False,
    )
```
